512 devices in a mesh: tile: 64 (over x, z, core), red: 8 (over y).
Axes of the slice: x: 4, y: 8, z: 8, core: 2. Of those that a mesh axis runs over, the one named last changes fastest.
Arguments:
- amplitudes: bfloat16 [16, 64, 1024, 1024], P('red', None, 'tile'), may hold values from -6 to 6
- intermediate: bfloat16 [1024, 16, 1024], P(None, 'red'), may hold values from -0.09375 to 0.09375
- contract_irrep: int32 [16], P('red'), may hold values from 0 to 3
- column_irrep: int32 [64], replicated, may hold values from 0 to 3
- virtual_irrep: int32 [8], replicated, may hold values from 0 to 3, as said below
Outputs:
- cycle_residual: bfloat16 [1024, 64, 1024], P('red', 'tile')
The draws below stay inside these ranges and needn't reach their ends.
Inputs may be any that keep to these rules, and one draw needn't show every extreme that they name: `virtual_irrep`: the four irreps label 8 // 2, 2, 1 and 1 of the virtual tiles; which irrep has which count, and which tiles it labels, differ from draw to draw.
All inputs are finite; a program needn't handle non-finite values.
Results may differ from the reference program's by a relative error of at most 0.017.
Values may be sent and summed in bfloat16 or wider, within the bound.
A program may use at most 64 MiB of HBM per device.

```python
import jax
import jax.numpy as jnp
from jax import lax

TILE = 128
VIRT = 1024
K_DEV = 2
K_ALL = 16
J_ALL = 64
NTILES = 8
N_RED = 8


def draw_virtual_irrep(key, part):
    key = jax.random.fold_in(key, 11)
    irrep_key, shuffle_key = jax.random.split(key)
    positions = jnp.arange(NTILES, dtype=jnp.int32)
    tile_rank = (positions >= NTILES // 2).astype(jnp.int32) + (positions >= 3 * NTILES // 4).astype(jnp.int32) + (positions >= 7 * NTILES // 8).astype(jnp.int32)
    irreps = jax.random.permutation(irrep_key, 4).astype(jnp.int32)
    tile_shuffle = jax.random.permutation(shuffle_key, NTILES).astype(jnp.int32)
    return irreps[tile_rank[tile_shuffle]].astype(jnp.int32)


def set_ends(entries, stream_key, low, largest):
    longest = entries.shape.index(max(entries.shape))
    spots = []
    for shift in (0, 1):
        where = [jax.random.randint(jax.random.fold_in(stream_key, axis), (), 0, length) for axis, length in enumerate(entries.shape)]
        where[longest] = (where[longest] + shift) % entries.shape[longest]
        spots.append(tuple(where))
    return entries.at[spots[0]].set(low).at[spots[1]].set(largest)


def block_levels(own_key, shape, pieces, low, top_value):
    loudness = 1.0
    for axis_at, parts in pieces:
        steps = jax.random.uniform(jax.random.fold_in(jax.random.fold_in(own_key, 6), axis_at), (parts,), jnp.float32, low / len(pieces), top_value / len(pieces))
        loudness = loudness * jnp.repeat(jnp.exp(steps), shape[axis_at] // parts).reshape((-1,) + (1,) * (len(shape) - 1 - axis_at))
    return loudness


def gaussian(rng, shape, spread, most, cuts=(), kind=jnp.bfloat16):
    values = jax.random.normal(rng, shape, jnp.float32) * spread
    if len(cuts) > 0:
        values = block_levels(rng, shape, cuts, -0.22, 0.18) * values
    return jnp.clip(values, min=-most, max=most).astype(kind)


def setup_inputs(seed: int = 0) -> dict:
    key_of = jax.random.split(jax.random.key(seed), 6)
    amplitudes = gaussian(key_of[0], (K_ALL, J_ALL, VIRT, VIRT), 1.0, 6.0, ((0, 8), (2, 64)))
    intermediate = gaussian(key_of[1], (VIRT, K_ALL, VIRT), (K_ALL * VIRT // 4) ** -0.5, 0.09375, ((1, 8),))
    contract_irrep = set_ends(jax.random.randint(key_of[2], (K_ALL,), 0, 4), jax.random.fold_in(key_of[2], 1), 0, 3).astype(jnp.int32)
    column_irrep = set_ends(jax.random.randint(key_of[3], (J_ALL,), 0, 4), jax.random.fold_in(key_of[3], 1), 0, 3).astype(jnp.int32)
    virtual_irrep = draw_virtual_irrep(jax.random.fold_in(key_of[5], 71), 0)
    return {"amplitudes": amplitudes, "intermediate": intermediate, "contract_irrep": contract_irrep, "column_irrep": column_irrep, "virtual_irrep": virtual_irrep}


def reference(amplitudes, intermediate, contract_irrep, column_irrep, virtual_irrep):
    tile_labels = jnp.repeat(virtual_irrep, TILE)

    def one_group(total, group):
        first = (group * K_DEV).astype(jnp.int32)
        block_amp = lax.dynamic_slice_in_dim(amplitudes, first, K_DEV, 0)
        block_irrep = lax.dynamic_slice_in_dim(contract_irrep, first, K_DEV, 0)
        block_weight = lax.dynamic_slice_in_dim(intermediate, first, K_DEV, 1)
        label = jnp.bitwise_xor(jnp.bitwise_xor(block_irrep[:, None, None, None], column_irrep[None, :, None, None]),
                                jnp.bitwise_xor(tile_labels[None, None, :, None], tile_labels[None, None, None, :]))
        masked = jnp.where(label == 0, block_amp, jnp.zeros_like(block_amp))
        product = jnp.einsum('akc,kjcb->ajb', block_weight.astype(jnp.float32), masked.astype(jnp.float32))
        rounded = lax.optimization_barrier(product.astype(jnp.bfloat16))
        return total + rounded.astype(jnp.float32), None

    start_total = jnp.zeros((VIRT, J_ALL, VIRT), jnp.float32)
    total, unused = lax.scan(one_group, start_total, jnp.arange(N_RED, dtype=jnp.int32))
    label_out = jnp.bitwise_xor(jnp.bitwise_xor(tile_labels[:, None, None], column_irrep[None, :, None]),
                                tile_labels[None, None, :])
    return jnp.where(label_out == 0, total, 0.0).astype(jnp.bfloat16)
```

```python
import functools

import jax
import jax.numpy as jnp
from jax import lax
from jax.experimental import pallas as pl
from jax.experimental.pallas import tpu as pltpu
from jax.sharding import PartitionSpec as P

TILE = 128
SLOTS = 4
CHUNKS = 4
MESH = pl.DeviceIdType.MESH


def peer(me, n, dims):
    xs, zs, cs = dims
    core, z, x = me % cs, (me // cs) % zs, me // (cs * zs)
    m = n % zs
    dz = ((m + 1) // 2) * (2 * (m % 2) - 1) + zs
    rest = n // zs
    dcore, dx = rest % cs, rest // cs
    return ((x + dx) % xs * zs + (z + dz) % zs) * cs + (core + dcore) % cs


def tile_ranks(lv, ntiles):
    labels = [lv[v] for v in range(ntiles)]
    ranks = []
    for v in range(ntiles):
        rank = jnp.int32(0)
        for u in range(v):
            rank = rank + jnp.where(labels[u] == labels[v], 1, 0)
        ranks.append(rank)
    return labels, ranks


def pack_kernel(ck, cj, lv, where, t, out, tab):
    n_k, n_j, rows, width = t.shape
    per = SLOTS // CHUNKS

    @pl.when(pl.program_id(0) == 0)
    def _():
        labels, ranks = tile_ranks(lv, width // TILE)
        for s in range(4):
            for i in range(SLOTS):
                pos = jnp.int32(0)
                for v in range(width // TILE):
                    pos = jnp.where((labels[v] == s) & (ranks[v] == i), v, pos)
                tab[s * SLOTS + i] = pos

    own_label = lv[where[0]]

    def step(j, carry):
        for k in range(n_k):
            s = ck[k] ^ cj[pl.program_id(0) * n_j + j] ^ own_label
            for i in range(SLOTS):
                tile = tab[s * SLOTS + i]
                q = i % per
                out[i // per, j, k, :, q * TILE:(q + 1) * TILE] = t[
                    k, j, :, pl.ds(pl.multiple_of(tile * TILE, TILE), TILE)]
        return carry

    lax.fori_loop(0, n_j, step, 0, unroll=4)


def unpack_kernel(cj, lv, where, packed, out):
    ntiles = out.shape[1] // TILE
    labels, ranks = tile_ranks(lv, ntiles)
    want = lv[where[1]] ^ cj[where[0]]
    for v in range(ntiles):
        block = packed[:, pl.ds(pl.multiple_of(ranks[v] * TILE, TILE), TILE)]
        keep = jnp.broadcast_to(labels[v] == want, block.shape)
        out[:, v * TILE:(v + 1) * TILE] = jnp.where(keep, block, jnp.zeros_like(block))


def kernel(dims, n_tile, n_red, pk, w_hbm, out, wv, recv, part, ybuf,
           w_sem, send_sem, recv_sem, own_sem, ysend_sem, yrecv_sem):
    me, my = lax.axis_index("tile"), lax.axis_index("red")
    n_k, rows = pk.shape[2], pk.shape[3]
    width = wv.shape[0]
    cw = pk.shape[4]
    w_copy = pltpu.make_async_copy(w_hbm, wv, w_sem)
    w_copy.start()

    barrier = pltpu.get_barrier_semaphore()

    def greet(n, carry):
        pl.semaphore_signal(barrier, inc=1, device_id=(peer(me, n, dims), my), device_id_type=MESH)
        return carry

    def greet_red(n, carry):
        pl.semaphore_signal(barrier, inc=1, device_id=(me, (my + n) % n_red), device_id_type=MESH)
        return carry

    lax.fori_loop(1, n_tile, greet, 0)
    lax.fori_loop(1, n_red, greet_red, 0)
    pl.semaphore_wait(barrier, n_tile + n_red - 2)

    own_rows = pl.ds(pl.multiple_of(me * rows, rows), rows)
    own = []
    for i in range(CHUNKS):
        def step(n, carry, i=i):
            j = peer(me, n, dims)
            pltpu.make_async_remote_copy(
                src_ref=pk.at[i, j],
                dst_ref=recv.at[i, :, own_rows, :],
                send_sem=send_sem.at[i],
                recv_sem=recv_sem.at[i],
                device_id=(j, my),
                device_id_type=MESH,
            ).start()
            return carry
        lax.fori_loop(1, n_tile, step, 0)
        copy = pltpu.make_async_copy(pk.at[i, me], recv.at[i, :, own_rows, :], own_sem.at[i])
        copy.start()
        own.append(copy)

    w_copy.wait()
    for i in range(CHUNKS):
        own[i].wait()
        others = recv.at[i, :, pl.ds(0, (n_tile - 1) * rows), :]
        pltpu.make_async_copy(others, others, recv_sem.at[i]).wait()

        def multiply(n, carry, i=i):
            to = (my + n) % n_red
            a_rows = pl.ds(pl.multiple_of(to * TILE, TILE), TILE)
            acc = jnp.dot(wv[a_rows, :width], recv[i, 0], preferred_element_type=jnp.float32)
            for k in range(1, n_k):
                acc += jnp.dot(wv[a_rows, k * width:(k + 1) * width], recv[i, k],
                               preferred_element_type=jnp.float32)
            part[i, to] = acc.astype(part.dtype)

            @pl.when(n < n_red)
            def _():
                pltpu.make_async_remote_copy(
                    src_ref=part.at[i, to],
                    dst_ref=ybuf.at[i, my],
                    send_sem=ysend_sem.at[i],
                    recv_sem=yrecv_sem.at[i],
                    device_id=(me, to),
                    device_id_type=MESH,
                ).start()
            return carry

        lax.fori_loop(1, n_red + 1, multiply, 0)

    for i in range(CHUNKS):
        others = ybuf.at[i, pl.ds(0, n_red - 1)]
        pltpu.make_async_copy(others, others, yrecv_sem.at[i]).wait()
        total = part[i, my].astype(jnp.float32)
        for d in range(1, n_red):
            total += ybuf[i, (my + d) % n_red].astype(jnp.float32)
        out[:, i * cw:(i + 1) * cw] = total.astype(out.dtype)

    for i in range(CHUNKS):
        sent = pk.at[i, pl.ds(0, n_tile - 1)]
        pltpu.make_async_copy(sent, sent, send_sem.at[i]).wait()
        sent = part.at[i, pl.ds(0, n_red - 1)]
        pltpu.make_async_copy(sent, sent, ysend_sem.at[i]).wait()


def local(n_tile, n_red, amplitudes, intermediate, contract_irrep, column_irrep, virtual_irrep):
    n_k, n_j, rows, width = amplitudes.shape
    me, my = lax.axis_index("tile"), lax.axis_index("red")
    dims = (4, 8, 2) if n_tile == 64 else (1, n_tile // 2, 2)
    cw = SLOTS // CHUNKS * TILE
    bf = jnp.bfloat16
    smem = pl.BlockSpec(memory_space=pltpu.SMEM)
    hbm = pl.BlockSpec(memory_space=pl.ANY)
    vmem = pl.BlockSpec(memory_space=pltpu.VMEM)

    group = 8
    packed = pl.pallas_call(
        pack_kernel,
        out_shape=jax.ShapeDtypeStruct((CHUNKS, n_j, n_k, rows, cw), bf),
        grid=(n_j // group,),
        in_specs=[smem, smem, smem, smem, pl.BlockSpec((n_k, group, rows, width), lambda g: (0, g, 0, 0))],
        out_specs=pl.BlockSpec((CHUNKS, group, n_k, rows, cw), lambda g: (0, g, 0, 0, 0)),
        scratch_shapes=[pltpu.SMEM((4 * SLOTS,), jnp.int32)],
    )(contract_irrep, column_irrep, virtual_irrep, jnp.reshape(me * rows // TILE, (1,)), amplitudes)

    tile_labels = jnp.repeat(virtual_irrep, TILE)
    label = tile_labels[:, None, None] ^ contract_irrep[None, :, None] ^ tile_labels[None, None, :]
    weight = jnp.where(label == 0, intermediate, jnp.zeros_like(intermediate)).reshape(width, n_k * width)

    summed = pl.pallas_call(
        functools.partial(kernel, dims, n_tile, n_red),
        out_shape=jax.ShapeDtypeStruct((TILE, SLOTS * TILE), bf),
        in_specs=[hbm, hbm],
        out_specs=vmem,
        scratch_shapes=[
            pltpu.VMEM((width, n_k * width), bf),
            pltpu.VMEM((CHUNKS, n_k, width, cw), bf),
            pltpu.VMEM((CHUNKS, n_red, TILE, cw), bf),
            pltpu.VMEM((CHUNKS, n_red, TILE, cw), bf),
            pltpu.SemaphoreType.DMA,
            pltpu.SemaphoreType.DMA((CHUNKS,)),
            pltpu.SemaphoreType.DMA((CHUNKS,)),
            pltpu.SemaphoreType.DMA((CHUNKS,)),
            pltpu.SemaphoreType.DMA((CHUNKS,)),
            pltpu.SemaphoreType.DMA((CHUNKS,)),
        ],
        compiler_params=pltpu.CompilerParams(
            collective_id=0, has_side_effects=True, vmem_limit_bytes=48 * 2**20
        ),
        cost_estimate=pl.CostEstimate(flops=2 * width**2 * n_k * SLOTS * TILE, bytes_accessed=9 * 2**20,
                                      transcendentals=0),
    )(packed, weight)

    out = pl.pallas_call(
        unpack_kernel,
        out_shape=jax.ShapeDtypeStruct((TILE, width), bf),
        in_specs=[smem, smem, smem, vmem],
        out_specs=vmem,
    )(column_irrep, virtual_irrep, jnp.stack([me, my]), summed)
    return out[:, None, :]


def solution(mesh):
    in_specs = (P("red", None, "tile", None), P(None, "red", None), P("red"), P(), P())
    out_specs = P("red", "tile", None)
    body = functools.partial(local, mesh.shape["tile"], mesh.shape["red"])
    return jax.shard_map(body, mesh=mesh, in_specs=in_specs, out_specs=out_specs, check_vma=False)
```

```python
import functools

import jax
import jax.numpy as jnp
from jax import lax
from jax.experimental import pallas as pl
from jax.experimental.pallas import tpu as pltpu
from jax.sharding import PartitionSpec as P

TILE = 128
SLOTS = 4
CHUNKS = 4
HALVED = 2
ORDER = (("multiply", 0), ("multiply", 1), ("cross", 0), ("multiply", 2), ("cross", 1), ("multiply", 3),
         ("finish", 0), ("finish", 1), ("finish", 2), ("finish", 3))
MESH = pl.DeviceIdType.MESH


def peer(me, n, dims):
    xs, zs, cs = dims
    core, z, x = me % cs, (me // cs) % zs, me // (cs * zs)
    m = n % zs
    dz = ((m + 1) // 2) * (2 * (m % 2) - 1) + zs
    rest = n // zs
    dcore, dx = rest % cs, rest // cs
    return ((x + dx) % xs * zs + (z + dz) % zs) * cs + (core + dcore) % cs


def tile_ranks(lv, ntiles):
    labels = [lv[v] for v in range(ntiles)]
    ranks = []
    for v in range(ntiles):
        rank = jnp.int32(0)
        for u in range(v):
            rank = rank + jnp.where(labels[u] == labels[v], 1, 0)
        ranks.append(rank)
    return labels, ranks


def pack_kernel(ck, cj, lv, where, t, out, keep, tab):
    n_k, n_j, rows, width = t.shape
    per = SLOTS // CHUNKS
    ntiles = width // TILE

    @pl.when(pl.program_id(0) == 0)
    def _():
        labels, ranks = tile_ranks(lv, width // TILE)
        for s in range(4):
            for i in range(SLOTS):
                pos = jnp.int32(0)
                for v in range(width // TILE):
                    pos = jnp.where((labels[v] == s) & (ranks[v] == i), v, pos)
                tab[s * SLOTS + i] = pos
        for a in range(ntiles):
            for k in range(n_k):
                for c in range(ntiles):
                    fits = jnp.where(labels[a] ^ labels[c] == ck[k], 1.0, 0.0)
                    keep[a, k:k + 1, c * TILE:(c + 1) * TILE] = jnp.full((1, TILE), fits, jnp.float32)

    own_label = lv[where[0]]

    def step(j, carry):
        for k in range(n_k):
            s = ck[k] ^ cj[pl.program_id(0) * n_j + j] ^ own_label
            for i in range(SLOTS):
                tile = tab[s * SLOTS + i]
                q = i % per
                out[i // per, j, k, :, q * TILE:(q + 1) * TILE] = t[
                    k, j, :, pl.ds(pl.multiple_of(tile * TILE, TILE), TILE)]
        return carry

    lax.fori_loop(0, n_j, step, 0, unroll=4)


def unpack_kernel(cj, lv, where, packed, out):
    ntiles = out.shape[1] // TILE
    labels, ranks = tile_ranks(lv, ntiles)
    want = lv[where[1]] ^ cj[where[0]]
    for v in range(ntiles):
        block = packed[:, pl.ds(pl.multiple_of(ranks[v] * TILE, TILE), TILE)]
        keep = jnp.broadcast_to(labels[v] == want, block.shape)
        out[:, v * TILE:(v + 1) * TILE] = jnp.where(keep, block, jnp.zeros_like(block))


def kernel(dims, n_tile, n_red, pk, w_hbm, keep, out, wraw, wv, recv_h, recv_d, part_h, part_d, ybuf_h, ybuf_d, mine, theirs, mbuf,
           w_sem, send_sem, recv_sem, own_sem, ysend_sem, yrecv_sem, msend_sem, mrecv_sem):
    xs, zs, cs = dims
    me, my = lax.axis_index("tile"), lax.axis_index("red")
    n_k, rows = pk.shape[2], pk.shape[3]
    width = wv.shape[1]
    half = zs // 2
    core, z, x = me % cs, (me // cs) % zs, me // (cs * zs)
    partner = (x * zs + (z + half) % zs) * cs + core
    w_copy = pltpu.make_async_copy(w_hbm, wraw, w_sem)
    w_copy.start()

    barrier = pltpu.get_barrier_semaphore()

    def greet(n, carry):
        pl.semaphore_signal(barrier, inc=1, device_id=(peer(me, n, dims), my), device_id_type=MESH)
        return carry

    def greet_red(n, carry):
        pl.semaphore_signal(barrier, inc=1, device_id=(me, (my + n) % n_red), device_id_type=MESH)
        return carry

    lax.fori_loop(1, n_tile, greet, 0)
    lax.fori_loop(1, n_red, greet_red, 0)

    def clear(n, carry):
        first = ((n // half) * zs + (z + half - 2 + core + n % half) % zs) * cs * rows
        where = pl.ds(pl.multiple_of(first, cs * rows), cs * rows)
        for i in range(HALVED):
            for k in range(n_k):
                recv_h[i, k, where, :] = jnp.zeros((cs * rows, 2 * TILE), recv_h.dtype)
        return carry

    lax.fori_loop(0, xs * half, clear, 0)
    pl.semaphore_wait(barrier, n_tile + n_red - 2)

    own_rows = pl.ds(pl.multiple_of(me * rows, rows), rows)
    own = []

    def step_h(n, carry, i):
        j = peer(me, n, dims)
        j_core, j_z, j_x = j % cs, (j // cs) % zs, j // (cs * zs)
        across = ((z - j_z + 2 - j_core + zs) % zs) // half
        to = (j_x * zs + (j_z + across * half) % zs) * cs + j_core
        pltpu.make_async_remote_copy(
            src_ref=pk.at[i, j],
            dst_ref=recv_h.at[i, :, own_rows, pl.ds(pl.multiple_of(across * TILE, TILE), TILE)],
            send_sem=send_sem.at[i],
            recv_sem=recv_sem.at[i],
            device_id=(to, my),
            device_id_type=MESH,
        ).start()
        return carry

    def step_d(n, carry, i):
        j = peer(me, n, dims)
        pltpu.make_async_remote_copy(
            src_ref=pk.at[i, j],
            dst_ref=recv_d.at[i - HALVED, :, own_rows, :],
            send_sem=send_sem.at[i],
            recv_sem=recv_sem.at[i],
            device_id=(j, my),
            device_id_type=MESH,
        ).start()
        return carry

    for i in range(CHUNKS):
        if i < HALVED:
            lax.fori_loop(1, zs - 1, functools.partial(step_h, i=i), 0)
            lax.fori_loop(zs, n_tile, functools.partial(step_h, i=i), 0)
            copies = [
                pltpu.make_async_copy(pk.at[i, me], recv_h.at[i, :, own_rows, pl.ds(0, TILE)], own_sem.at[i, 0]),
                pltpu.make_async_copy(pk.at[i, partner], recv_h.at[i, :, own_rows, pl.ds(TILE, TILE)], own_sem.at[i, 1]),
            ]
        else:
            lax.fori_loop(1, n_tile, functools.partial(step_d, i=i), 0)
            copies = [pltpu.make_async_copy(pk.at[i, me], recv_d.at[i - HALVED, :, own_rows, :], own_sem.at[i, 0])]
        for copy in copies:
            copy.start()
        own.append(copies)

    w_copy.wait()
    row = lax.broadcasted_iota(jnp.int32, (TILE, n_k * TILE), 0)
    col = lax.broadcasted_iota(jnp.int32, (TILE, n_k * TILE), 1)
    picks = [jnp.where(col == n_k * row + k, 1.0, 0.0).astype(wv.dtype) for k in range(n_k)]

    def arrange(a, carry):
        a_rows = pl.ds(pl.multiple_of(a * TILE, TILE), TILE)
        pairs = wraw[a_rows].reshape(n_k * TILE, width)
        for k in range(n_k):
            plane = jnp.dot(picks[k], pairs, preferred_element_type=jnp.float32)
            wv[k, a_rows, :] = (plane * keep[a, k:k + 1, :]).astype(wv.dtype)
        return carry

    lax.fori_loop(0, n_red, arrange, 0)

    def multiply(i):
        for copy in own[i]:
            copy.wait()
        if i < HALVED:
            got, part, ybuf, at, n_got = recv_h, part_h, ybuf_h, i, n_tile - 2
        else:
            got, part, ybuf, at, n_got = recv_d, part_d, ybuf_d, i - HALVED, n_tile - 1
        others = got.at[at, :, pl.ds(0, n_got * rows), pl.ds(0, TILE)]
        pltpu.make_async_copy(others, others, recv_sem.at[i]).wait()

        def block(n, carry):
            to = (my + n) % n_red
            a_rows = pl.ds(pl.multiple_of(to * TILE, TILE), TILE)
            acc = jnp.dot(wv[0, a_rows, :], got[at, 0], preferred_element_type=jnp.float32)
            for k in range(1, n_k):
                acc += jnp.dot(wv[k, a_rows, :], got[at, k], preferred_element_type=jnp.float32)
            part[at, to] = acc.astype(part.dtype)

            @pl.when(n < n_red)
            def _():
                pltpu.make_async_remote_copy(
                    src_ref=part.at[at, to],
                    dst_ref=ybuf.at[at, my],
                    send_sem=ysend_sem.at[i],
                    recv_sem=yrecv_sem.at[i],
                    device_id=(me, to),
                    device_id_type=MESH,
                ).start()
            return carry

        lax.fori_loop(1, n_red + 1, block, 0)

    def add_up(i):
        part, ybuf, at = (part_h, ybuf_h, i) if i < HALVED else (part_d, ybuf_d, i - HALVED)
        others = ybuf.at[at, pl.ds(0, n_red - 1)]
        pltpu.make_async_copy(others, others, yrecv_sem.at[i]).wait()
        total = part[at, my].astype(jnp.float32)
        for d in range(1, n_red):
            total += ybuf[at, (my + d) % n_red].astype(jnp.float32)
        return total

    crossing = []

    def cross(i):
        total = add_up(i)
        mine[i] = total[:, :TILE]
        theirs[i] = total[:, TILE:].astype(theirs.dtype)
        copy = pltpu.make_async_remote_copy(
            src_ref=theirs.at[i], dst_ref=mbuf.at[i], send_sem=msend_sem.at[i], recv_sem=mrecv_sem.at[i],
            device_id=(partner, my), device_id_type=MESH)
        copy.start()
        crossing.append(copy)

    def finish(i):
        if i < HALVED:
            crossing[i].wait_recv()
            total = mine[i] + mbuf[i].astype(jnp.float32)
        else:
            total = add_up(i)
        out[:, i * TILE:(i + 1) * TILE] = total.astype(out.dtype)

    for kind, i in ORDER:
        {"multiply": multiply, "cross": cross, "finish": finish}[kind](i)

    for i in range(CHUNKS):
        at = i if i < HALVED else i - HALVED
        sent = pk.at[i, pl.ds(0, n_tile - 2 if i < HALVED else n_tile - 1)]
        pltpu.make_async_copy(sent, sent, send_sem.at[i]).wait()
        sent = (part_h if i < HALVED else part_d).at[at, pl.ds(0, n_red - 1)]
        pltpu.make_async_copy(sent, sent, ysend_sem.at[i]).wait()
    for copy in crossing:
        copy.wait_send()


def local(n_tile, n_red, amplitudes, intermediate, contract_irrep, column_irrep, virtual_irrep):
    n_k, n_j, rows, width = amplitudes.shape
    me, my = lax.axis_index("tile"), lax.axis_index("red")
    dims = (4, 8, 2) if n_tile == 64 else (1, n_tile // 2, 2)
    cw = SLOTS // CHUNKS * TILE
    bf = jnp.bfloat16
    smem = pl.BlockSpec(memory_space=pltpu.SMEM)
    hbm = pl.BlockSpec(memory_space=pl.ANY)
    vmem = pl.BlockSpec(memory_space=pltpu.VMEM)

    group = 8
    ntiles = width // TILE
    packed, keep = pl.pallas_call(
        pack_kernel,
        out_shape=(jax.ShapeDtypeStruct((CHUNKS, n_j, n_k, rows, cw), bf),
                   jax.ShapeDtypeStruct((ntiles, n_k, width), jnp.float32)),
        grid=(n_j // group,),
        in_specs=[smem, smem, smem, smem, pl.BlockSpec((n_k, group, rows, width), lambda g: (0, g, 0, 0))],
        out_specs=(pl.BlockSpec((CHUNKS, group, n_k, rows, cw), lambda g: (0, g, 0, 0, 0)),
                   pl.BlockSpec((ntiles, n_k, width), lambda g: (0, 0, 0))),
        scratch_shapes=[pltpu.SMEM((4 * SLOTS,), jnp.int32)],
    )(contract_irrep, column_irrep, virtual_irrep, jnp.reshape(me * rows // TILE, (1,)), amplitudes)

    summed = pl.pallas_call(
        functools.partial(kernel, dims, n_tile, n_red),
        out_shape=jax.ShapeDtypeStruct((TILE, SLOTS * TILE), bf),
        in_specs=[hbm, hbm, vmem],
        out_specs=vmem,
        scratch_shapes=[
            pltpu.VMEM((width, n_k, width), bf),
            pltpu.VMEM((n_k, width, width), bf),
            pltpu.VMEM((HALVED, n_k, width, 2 * TILE), bf),
            pltpu.VMEM((CHUNKS - HALVED, n_k, width, TILE), bf),
            pltpu.VMEM((HALVED, n_red, TILE, 2 * TILE), bf),
            pltpu.VMEM((CHUNKS - HALVED, n_red, TILE, TILE), bf),
            pltpu.VMEM((HALVED, n_red, TILE, 2 * TILE), bf),
            pltpu.VMEM((CHUNKS - HALVED, n_red, TILE, TILE), bf),
            pltpu.VMEM((HALVED, TILE, TILE), jnp.float32),
            pltpu.VMEM((HALVED, TILE, TILE), bf),
            pltpu.VMEM((HALVED, TILE, TILE), bf),
            pltpu.SemaphoreType.DMA,
            pltpu.SemaphoreType.DMA((CHUNKS,)),
            pltpu.SemaphoreType.DMA((CHUNKS,)),
            pltpu.SemaphoreType.DMA((CHUNKS, 2)),
            pltpu.SemaphoreType.DMA((CHUNKS,)),
            pltpu.SemaphoreType.DMA((CHUNKS,)),
            pltpu.SemaphoreType.DMA((HALVED,)),
            pltpu.SemaphoreType.DMA((HALVED,)),
        ],
        compiler_params=pltpu.CompilerParams(
            collective_id=0, has_side_effects=True, vmem_limit_bytes=48 * 2**20
        ),
        cost_estimate=pl.CostEstimate(flops=2 * width**2 * n_k * SLOTS * TILE, bytes_accessed=9 * 2**20,
                                      transcendentals=0),
    )(packed, intermediate, keep)

    out = pl.pallas_call(
        unpack_kernel,
        out_shape=jax.ShapeDtypeStruct((TILE, width), bf),
        in_specs=[smem, smem, smem, vmem],
        out_specs=vmem,
    )(column_irrep, virtual_irrep, jnp.stack([me, my]), summed)
    return out[:, None, :]


def solution(mesh):
    in_specs = (P("red", None, "tile", None), P(None, "red", None), P("red"), P(), P())
    out_specs = P("red", "tile", None)
    body = functools.partial(local, mesh.shape["tile"], mesh.shape["red"])
    return jax.shard_map(body, mesh=mesh, in_specs=in_specs, out_specs=out_specs, check_vma=False)
```

```python
import functools

import jax
import jax.numpy as jnp
from jax import lax
from jax.experimental import pallas as pl
from jax.experimental.pallas import tpu as pltpu
from jax.sharding import PartitionSpec as P

TILE = 128
SLOTS = 4
HALVED = (0, 1, 2)
RING = (0, 1, 2)
ORDER = (
    ("multiply", 0), ("ring", 0, 2), ("multiply", 1), ("ring", 0, 3), ("ring", 1, 2),
    ("ring", 0, 4), ("multiply", 2), ("ring", 1, 3), ("cross", 0), ("ring", 2, 2),
    ("ring", 1, 4), ("ring", 2, 3), ("cross", 1), ("ring", 2, 4), ("cross", 2),
    ("multiply", 3), ("finish", 0), ("finish", 1), ("finish", 2), ("finish", 3),
)
MESH = pl.DeviceIdType.MESH


def wrap(value, size):
    return jnp.where(value >= size, value - size, value)


def tile_codes(lv, ntiles):
    codes = []
    for v in range(ntiles):
        code = lv[v] * 8
        for u in range(v):
            code = code + (lv[u] == lv[v]).astype(jnp.int32)
        codes.append(code)
    return codes


def kernel(dims, n_tile, n_red, ck, cj, lv, t_hbm, w_hbm, out, tv, wraw, wv, lanes, pk, recv, part, ybuf, mine, theirs, mbuf, sums,
           t_sem, w_sem, send_sem, recv_sem, own_sem, ysend_sem, yrecv_sem, msend_sem, mrecv_sem):
    xs, zs, cs = dims
    me, my = lax.axis_index("tile"), lax.axis_index("red")
    n_k, n_j, rows, width = tv.shape
    ntiles = width // TILE
    half, halfway = zs // 2, n_red // 2
    core, z, x = me % cs, (me // cs) % zs, me // (cs * zs)
    partner = (x * zs + wrap(z + half, zs)) * cs + core

    steps = [(dcore, dz) for dcore in range(cs) for dz in (0, 1, zs - 1, 2, zs - 2, 3, zs - 3, half)]
    places, homes = [], []
    for dcore, dz in steps:
        j_core, j_z = wrap(core + dcore, cs), wrap(z + dz, zs)
        behind = wrap(zs - dz + 2 - j_core, zs)
        across = jnp.where(behind >= half, 1, 0)
        places.append(j_z * cs + j_core)
        homes.append((wrap(j_z + half * across, zs) * cs + j_core, across))

    def each_peer(visit, skip):
        for q in range(len(steps)):
            if steps[q] not in skip:
                visit(x * zs * cs, q)

        def plane(dx, carry):
            for q in range(len(steps)):
                visit(wrap(x + dx, xs) * zs * cs, q)
            return carry

        lax.fori_loop(1, xs, plane, 0)

    t_copy = pltpu.make_async_copy(t_hbm, tv, t_sem)
    t_copy.start()
    w_copy = pltpu.make_async_copy(w_hbm, wraw, w_sem)
    w_copy.start()

    barrier = pltpu.get_barrier_semaphore()

    def greet(base, q):
        pl.semaphore_signal(barrier, inc=1, device_id=(base + places[q], my), device_id_type=MESH)

    each_peer(greet, [(0, 0)])
    for d in range(1, n_red):
        pl.semaphore_signal(barrier, inc=1, device_id=(me, wrap(my + d, n_red)), device_id_type=MESH)

    def clear(n, carry):
        for far in range(half):
            first = (n * zs + wrap(z + wrap(half - 2 + core + far, zs), zs)) * cs * rows
            where = pl.ds(pl.multiple_of(first, cs * rows), cs * rows)
            for i in HALVED:
                for k in range(n_k):
                    recv[i][k, where, :] = jnp.zeros((cs * rows, 2 * TILE), recv[i].dtype)
        return carry

    lax.fori_loop(0, xs, clear, 0)

    codes = tile_codes(lv, ntiles)
    own_label = lv[me * rows // TILE]
    for c in range(ntiles):
        lanes[:, c * TILE:(c + 1) * TILE] = jnp.full((8, TILE), lv[c], jnp.int32)
    t_copy.wait()

    def pack(j, carry):
        for k in range(n_k):
            key = jnp.full((rows, TILE), (ck[k] ^ cj[j] ^ own_label) * 8, jnp.int32)
            tiles = [tv[k, j, :, v * TILE:(v + 1) * TILE].astype(jnp.float32) for v in range(ntiles)]
            for i in range(SLOTS):
                found = tiles[i]
                for v in range(i + 1, ntiles):
                    found = jnp.where(key == codes[v] - i, tiles[v], found)
                pk[i, j, k] = found.astype(pk.dtype)
        return carry

    lax.fori_loop(0, n_j, pack, 0)
    pl.semaphore_wait(barrier, n_tile + n_red - 2)

    own_rows = pl.ds(pl.multiple_of(me * rows, rows), rows)
    own = []

    def send(i, base, q):
        place, (home, across) = places[q], homes[q]
        if i in HALVED:
            to = base + home
            columns = pl.ds(pl.multiple_of(across * TILE, TILE), TILE)
        else:
            to = base + place
            columns = pl.ds(0, TILE)
        pltpu.make_async_remote_copy(
            src_ref=pk.at[i, base + place],
            dst_ref=recv[i].at[:, own_rows, columns],
            send_sem=send_sem.at[i],
            recv_sem=recv_sem.at[i],
            device_id=(to, my),
            device_id_type=MESH,
        ).start()

    for i in range(SLOTS):
        copies = [pltpu.make_async_copy(pk.at[i, me], recv[i].at[:, own_rows, pl.ds(0, TILE)], own_sem.at[i, 0])]
        if i in HALVED:
            each_peer(functools.partial(send, i), [(0, 0), (0, half)])
            copies.append(pltpu.make_async_copy(
                pk.at[i, partner], recv[i].at[:, own_rows, pl.ds(TILE, TILE)], own_sem.at[i, 1]))
        else:
            each_peer(functools.partial(send, i), [(0, 0)])
        for copy in copies:
            copy.start()
        own.append(copies)

    w_copy.wait()
    row = lax.broadcasted_iota(jnp.int32, (TILE, n_k * TILE), 0)
    col = lax.broadcasted_iota(jnp.int32, (TILE, n_k * TILE), 1)
    picks = [jnp.where(col == n_k * row + k, 1.0, 0.0).astype(wv.dtype) for k in range(n_k)]

    def arrange(a, carry):
        a_rows = pl.ds(pl.multiple_of(a * TILE, TILE), TILE)
        pairs = wraw[a_rows].reshape(n_k * TILE, width)
        for k in range(n_k):
            plane = jnp.dot(picks[k], pairs, preferred_element_type=jnp.float32)
            keep = jnp.broadcast_to(lanes[0:1, :], plane.shape) == jnp.full(plane.shape, lv[a] ^ ck[k], jnp.int32)
            wv[k, a_rows, :] = jnp.where(keep, plane, 0.0).astype(wv.dtype)
        return carry

    lax.fori_loop(0, ntiles, arrange, 0)

    def around(i, direction, t, block):
        return pltpu.make_async_remote_copy(
            src_ref=block,
            dst_ref=ybuf[i].at[direction * halfway + t - 1],
            send_sem=ysend_sem.at[i, direction * halfway + t - 1],
            recv_sem=yrecv_sem.at[i, direction * halfway + t - 1],
            device_id=(me, wrap(my + (1 if direction == 0 else n_red - 1), n_red)),
            device_id_type=MESH,
        )

    ring_copies = {}
    first_pair = wrap(my // 2 + n_red // 4, n_red // 2)

    def multiply(i):
        for copy in own[i]:
            copy.wait()
        n_got = n_tile - 2 if i in HALVED else n_tile - 1
        others = recv[i].at[:, pl.ds(0, n_got * rows), pl.ds(0, TILE)]
        pltpu.make_async_copy(others, others, recv_sem.at[i]).wait()

        def block(n, carry):
            pair = wrap(first_pair + n, n_red // 2)
            a_rows = pl.ds(pl.multiple_of(pair * 2 * TILE, 2 * TILE), 2 * TILE)
            acc = jnp.dot(wv[0, a_rows, :], recv[i][0], preferred_element_type=jnp.float32)
            for k in range(1, n_k):
                acc += jnp.dot(wv[k, a_rows, :], recv[i][k], preferred_element_type=jnp.float32)
            for h in range(2):
                to = pair * 2 + h
                part[i][to] = acc[h * TILE:(h + 1) * TILE].astype(part[i].dtype)

                if i not in RING:
                    @pl.when(to != my)
                    def _():
                        pltpu.make_async_remote_copy(
                            src_ref=part[i].at[to],
                            dst_ref=ybuf[i].at[my],
                            send_sem=ysend_sem.at[i, 0],
                            recv_sem=yrecv_sem.at[i, 0],
                            device_id=(me, to),
                            device_id_type=MESH,
                        ).start()
            return carry

        lax.fori_loop(0, n_red // 2, block, 0)
        if i in RING:
            ring_copies[i, 0, 1] = around(i, 0, 1, part[i].at[wrap(my + halfway, n_red)])
            ring_copies[i, 1, 1] = around(i, 1, 1, part[i].at[wrap(my + halfway + 1, n_red)])
            ring_copies[i, 0, 1].start()
            ring_copies[i, 1, 1].start()

    def ring(i, t):
        for direction in (0, 1):
            if direction == 1 and t == halfway:
                continue
            ring_copies[i, direction, t - 1].wait_recv()
            at = direction * halfway + t - 2
            ahead = (halfway + 1 - t) if direction == 0 else (n_red - halfway + t)
            total = part[i][wrap(my + ahead, n_red)].astype(jnp.float32) + ybuf[i][at].astype(jnp.float32)
            sums[i][at] = total.astype(sums[i].dtype)
            copy = around(i, direction, t, sums[i].at[at])
            copy.start()
            ring_copies[i, direction, t] = copy

    def add_up(i):
        total = part[i][my].astype(jnp.float32)
        if i in RING:
            ring_copies[i, 0, halfway].wait_recv()
            ring_copies[i, 1, halfway - 1].wait_recv()
            total += ybuf[i][halfway - 1].astype(jnp.float32)
            total += ybuf[i][2 * halfway - 2].astype(jnp.float32)
        else:
            others = ybuf[i].at[pl.ds(0, n_red - 1)]
            pltpu.make_async_copy(others, others, yrecv_sem.at[i, 0]).wait()
            for d in range(1, n_red):
                total += ybuf[i][wrap(my + d, n_red)].astype(jnp.float32)
        return total

    crossing = {}

    def cross(i):
        total = add_up(i)
        mine[i] = total[:, :TILE]
        theirs[i] = total[:, TILE:].astype(theirs.dtype)
        copy = pltpu.make_async_remote_copy(
            src_ref=theirs.at[i], dst_ref=mbuf.at[i], send_sem=msend_sem.at[i], recv_sem=mrecv_sem.at[i],
            device_id=(partner, my), device_id_type=MESH)
        copy.start()
        crossing[i] = copy

    def finish(i):
        if i in HALVED:
            crossing[i].wait_recv()
            mine[i] += mbuf[i].astype(jnp.float32)
        else:
            mine[i] = add_up(i)

    for kind, *where in ORDER:
        {"multiply": multiply, "ring": ring, "cross": cross, "finish": finish}[kind](*where)

    want = jnp.full((TILE, TILE), (lv[my] ^ cj[me]) * 8, jnp.int32)
    for v in range(ntiles):
        found = jnp.zeros((TILE, TILE), jnp.float32)
        for i in range(min(v + 1, SLOTS)):
            found = jnp.where(want == codes[v] - i, mine[i], found)
        out[:, v * TILE:(v + 1) * TILE] = found.astype(out.dtype)

    for i in range(SLOTS):
        sent = pk.at[i, pl.ds(0, n_tile - 2 if i in HALVED else n_tile - 1)]
        pltpu.make_async_copy(sent, sent, send_sem.at[i]).wait()
        if i not in RING:
            sent = part[i].at[pl.ds(0, n_red - 1)]
            pltpu.make_async_copy(sent, sent, ysend_sem.at[i, 0]).wait()
    for copy in list(ring_copies.values()) + list(crossing.values()):
        copy.wait_send()


def local(n_tile, n_red, amplitudes, intermediate, contract_irrep, column_irrep, virtual_irrep):
    n_k, n_j, rows, width = amplitudes.shape
    dims = (4, 8, 2)
    bf = jnp.bfloat16
    smem = pl.BlockSpec(memory_space=pltpu.SMEM)
    hbm = pl.BlockSpec(memory_space=pl.ANY)
    cols = [2 * TILE if i in HALVED else TILE for i in range(SLOTS)]
    blocks = [pltpu.VMEM((n_red, TILE, c), bf) for c in cols]
    out = pl.pallas_call(
        functools.partial(kernel, dims, n_tile, n_red),
        out_shape=jax.ShapeDtypeStruct((TILE, width), bf),
        in_specs=[smem, smem, smem, hbm, hbm],
        out_specs=pl.BlockSpec(memory_space=pltpu.VMEM),
        scratch_shapes=[
            pltpu.VMEM((n_k, n_j, rows, width), bf),
            pltpu.VMEM((width, n_k, width), bf),
            pltpu.VMEM((n_k, width, width), bf),
            pltpu.VMEM((8, width), jnp.int32),
            pltpu.VMEM((SLOTS, n_j, n_k, rows, TILE), bf),
            [pltpu.VMEM((n_k, width, c), bf) for c in cols],
            blocks,
            blocks,
            pltpu.VMEM((SLOTS, TILE, TILE), jnp.float32),
            pltpu.VMEM((SLOTS, TILE, TILE), bf),
            pltpu.VMEM((SLOTS, TILE, TILE), bf),
            blocks,
            pltpu.SemaphoreType.DMA,
            pltpu.SemaphoreType.DMA,
            pltpu.SemaphoreType.DMA((SLOTS,)),
            pltpu.SemaphoreType.DMA((SLOTS,)),
            pltpu.SemaphoreType.DMA((SLOTS, 2)),
            pltpu.SemaphoreType.DMA((SLOTS, n_red)),
            pltpu.SemaphoreType.DMA((SLOTS, n_red)),
            pltpu.SemaphoreType.DMA((SLOTS,)),
            pltpu.SemaphoreType.DMA((SLOTS,)),
        ],
        compiler_params=pltpu.CompilerParams(
            collective_id=0, has_side_effects=True, vmem_limit_bytes=48 * 2**20
        ),
        cost_estimate=pl.CostEstimate(flops=2 * width**2 * n_k * SLOTS * TILE, bytes_accessed=9 * 2**20,
                                      transcendentals=0),
    )(contract_irrep, column_irrep, virtual_irrep, amplitudes, intermediate)
    return out[:, None, :]


def solution(mesh):
    in_specs = (P("red", None, "tile", None), P(None, "red", None), P("red"), P(), P())
    out_specs = P("red", "tile", None)
    body = functools.partial(local, mesh.shape["tile"], mesh.shape["red"])
    return jax.shard_map(body, mesh=mesh, in_specs=in_specs, out_specs=out_specs, check_vma=False)
```

```python
import functools

import jax
import jax.numpy as jnp
from jax import lax
from jax.experimental import pallas as pl
from jax.experimental.pallas import tpu as pltpu
from jax.sharding import PartitionSpec as P

TILE = 128
SLOTS = 4
HALVED = (0, 1, 2)
TWO_STEP = (0, 1, 2, 3)
ORDER = (
    ("launch", 0), ("launch", 1), ("launch", 2), ("launch", 3), ("weights",),
    ("multiply", 0), ("combine", 0), ("multiply", 1), ("combine", 1), ("cross", 0),
    ("multiply", 2), ("combine", 2), ("cross", 1), ("multiply", 3), ("cross", 2),
    ("combine", 3), ("finish", 0), ("finish", 1), ("finish", 2), ("finish", 3),
)
MESH = pl.DeviceIdType.MESH


def wrap(value, size):
    return jnp.where(value >= size, value - size, value)


def tile_codes(lv, ntiles):
    codes = []
    for v in range(ntiles):
        code = lv[v] * 8
        for u in range(v):
            code = code + (lv[u] == lv[v]).astype(jnp.int32)
        codes.append(code)
    return codes


def kernel(dims, n_tile, n_red, ck, cj, lv, t_hbm, w_hbm, out, tv, wraw, wv, lanes, pk, recv, part, ybuf, mine, theirs, mbuf, sums,
           t_sem, w_sem, send_sem, recv_sem, own_sem, ysend_sem, yrecv_sem, msend_sem, mrecv_sem):
    xs, zs, cs = dims
    me, my = lax.axis_index("tile"), lax.axis_index("red")
    n_k, n_j, rows, width = tv.shape
    ntiles = width // TILE
    half = zs // 2
    core, z, x = me % cs, (me // cs) % zs, me // (cs * zs)
    partner = (x * zs + wrap(z + half, zs)) * cs + core

    steps = [(dcore, dz) for dcore in range(cs) for dz in (0, 1, zs - 1, 2, zs - 2, 3, zs - 3, half)]
    places, homes = [], []
    for dcore, dz in steps:
        j_core, j_z = wrap(core + dcore, cs), wrap(z + dz, zs)
        behind = wrap(zs - dz + 2 - j_core, zs)
        across = jnp.where(behind >= half, 1, 0)
        places.append(j_z * cs + j_core)
        homes.append((wrap(j_z + half * across, zs) * cs + j_core, across))

    def each_peer(visit, skip):
        for q in range(len(steps)):
            if steps[q] not in skip:
                visit(x * zs * cs, q)

        def plane(dx, carry):
            for q in range(len(steps)):
                visit(wrap(x + dx, xs) * zs * cs, q)
            return carry

        lax.fori_loop(1, xs, plane, 0)

    t_copy = pltpu.make_async_copy(t_hbm, tv, t_sem)
    t_copy.start()
    w_copy = pltpu.make_async_copy(w_hbm, wraw, w_sem)
    w_copy.start()

    barrier = pltpu.get_barrier_semaphore()

    def greet(base, q):
        pl.semaphore_signal(barrier, inc=1, device_id=(base + places[q], my), device_id_type=MESH)

    each_peer(greet, [(0, 0)])
    for d in range(1, n_red):
        pl.semaphore_signal(barrier, inc=1, device_id=(me, wrap(my + d, n_red)), device_id_type=MESH)

    def clear(n, carry):
        for far in range(half):
            first = (n * zs + wrap(z + wrap(half - 2 + core + far, zs), zs)) * cs * rows
            where = pl.ds(pl.multiple_of(first, cs * rows), cs * rows)
            for i in HALVED:
                for k in range(n_k):
                    recv[i][k, where, :] = jnp.zeros((cs * rows, 2 * TILE), recv[i].dtype)
        return carry

    lax.fori_loop(0, xs, clear, 0)

    codes = tile_codes(lv, ntiles)
    own_label = lv[me * rows // TILE]
    for c in range(ntiles):
        lanes[:, c * TILE:(c + 1) * TILE] = jnp.full((8, TILE), lv[c], jnp.int32)
    t_copy.wait()

    def pack(j, carry):
        for k in range(n_k):
            key = jnp.full((rows, TILE), (ck[k] ^ cj[j] ^ own_label) * 8, jnp.int32)
            tiles = [tv[k, j, :, v * TILE:(v + 1) * TILE].astype(jnp.float32) for v in range(ntiles)]
            for i in range(SLOTS):
                found = tiles[i]
                for v in range(i + 1, ntiles):
                    found = jnp.where(key == codes[v] - i, tiles[v], found)
                pk[i, j, k] = found.astype(pk.dtype)
        return carry

    lax.fori_loop(0, n_j, pack, 0)
    pl.semaphore_wait(barrier, n_tile + n_red - 2)

    own_rows = pl.ds(pl.multiple_of(me * rows, rows), rows)
    own = {}

    def send(i, base, q):
        place, (home, across) = places[q], homes[q]
        if i in HALVED:
            to = base + home
            columns = pl.ds(pl.multiple_of(across * TILE, TILE), TILE)
        else:
            to = base + place
            columns = pl.ds(0, TILE)
        pltpu.make_async_remote_copy(
            src_ref=pk.at[i, base + place],
            dst_ref=recv[i].at[:, own_rows, columns],
            send_sem=send_sem.at[i],
            recv_sem=recv_sem.at[i],
            device_id=(to, my),
            device_id_type=MESH,
        ).start()

    def launch(i):
        copies = [pltpu.make_async_copy(pk.at[i, me], recv[i].at[:, own_rows, pl.ds(0, TILE)], own_sem.at[i, 0])]
        if i in HALVED:
            each_peer(functools.partial(send, i), [(0, 0), (0, half)])
            copies.append(pltpu.make_async_copy(
                pk.at[i, partner], recv[i].at[:, own_rows, pl.ds(TILE, TILE)], own_sem.at[i, 1]))
        else:
            each_peer(functools.partial(send, i), [(0, 0)])
        for copy in copies:
            copy.start()
        own[i] = copies

    def weights():
        w_copy.wait()
        row = lax.broadcasted_iota(jnp.int32, (TILE, n_k * TILE), 0)
        col = lax.broadcasted_iota(jnp.int32, (TILE, n_k * TILE), 1)
        picks = [jnp.where(col == n_k * row + k, 1.0, 0.0).astype(wv.dtype) for k in range(n_k)]

        def arrange(a, carry):
            a_rows = pl.ds(pl.multiple_of(a * TILE, TILE), TILE)
            pairs = wraw[a_rows].reshape(n_k * TILE, width)
            for k in range(n_k):
                plane = jnp.dot(picks[k], pairs, preferred_element_type=jnp.float32)
                keep = jnp.broadcast_to(lanes[0:1, :], plane.shape) == jnp.full(plane.shape, lv[a] ^ ck[k], jnp.int32)
                wv[k, a_rows, :] = jnp.where(keep, plane, 0.0).astype(wv.dtype)
            return carry

        lax.fori_loop(0, ntiles, arrange, 0)

    def along(offset):
        offset = offset % n_red
        return wrap(my + jnp.where(core == 1, n_red - offset, offset), n_red)

    first_step = ((0, -3, -1), (1, 4, 2), (2, 3, 1), (3, -1, -1), (4, 1, 1))

    def hop(i, slot, block, offset):
        return pltpu.make_async_remote_copy(
            src_ref=block,
            dst_ref=ybuf[i].at[slot],
            send_sem=ysend_sem.at[i, slot],
            recv_sem=yrecv_sem.at[i, slot],
            device_id=(me, along(offset)),
            device_id_type=MESH,
        )

    hops = {}
    first_pair = wrap(my // 2 + n_red // 4, n_red // 2)

    def multiply(i):
        for copy in own[i]:
            copy.wait()
        n_got = n_tile - 2 if i in HALVED else n_tile - 1
        others = recv[i].at[:, pl.ds(0, n_got * rows), pl.ds(0, TILE)]
        pltpu.make_async_copy(others, others, recv_sem.at[i]).wait()

        def block(n, carry):
            pair = wrap(first_pair + n, n_red // 2)
            a_rows = pl.ds(pl.multiple_of(pair * 2 * TILE, 2 * TILE), 2 * TILE)
            acc = jnp.dot(wv[0, a_rows, :], recv[i][0], preferred_element_type=jnp.float32)
            for k in range(1, n_k):
                acc += jnp.dot(wv[k, a_rows, :], recv[i][k], preferred_element_type=jnp.float32)
            for h in range(2):
                to = pair * 2 + h
                part[i][to] = acc[h * TILE:(h + 1) * TILE].astype(part[i].dtype)

                if i not in TWO_STEP:
                    @pl.when(to != my)
                    def _():
                        pltpu.make_async_remote_copy(
                            src_ref=part[i].at[to],
                            dst_ref=ybuf[i].at[my],
                            send_sem=ysend_sem.at[i, 0],
                            recv_sem=yrecv_sem.at[i, 0],
                            device_id=(me, to),
                            device_id_type=MESH,
                        ).start()
            return carry

        lax.fori_loop(0, n_red // 2, block, 0)
        if i in TWO_STEP:
            for slot, to, by in first_step:
                hops[i, slot] = hop(i, slot, part[i].at[along(to)], by)
                hops[i, slot].start()

    def combine(i):
        for slot, to, parts in ((5, -2, (0,)), (6, 2, (1, 2))):
            total = part[i][along(to)].astype(jnp.float32)
            for p in parts:
                hops[i, p].wait_recv()
                total += ybuf[i][p].astype(jnp.float32)
            sums[i][slot] = total.astype(sums[i].dtype)
            hops[i, slot] = hop(i, slot, sums[i].at[slot], to)
            hops[i, slot].start()

    def add_up(i):
        total = part[i][my].astype(jnp.float32)
        if i in TWO_STEP:
            for slot in (3, 4, 5, 6):
                hops[i, slot].wait_recv()
                total += ybuf[i][slot].astype(jnp.float32)
        else:
            others = ybuf[i].at[pl.ds(0, n_red - 1)]
            pltpu.make_async_copy(others, others, yrecv_sem.at[i, 0]).wait()
            for d in range(1, n_red):
                total += ybuf[i][wrap(my + d, n_red)].astype(jnp.float32)
        return total

    crossing = {}

    def cross(i):
        total = add_up(i)
        mine[i] = total[:, :TILE]
        theirs[i] = total[:, TILE:].astype(theirs.dtype)
        copy = pltpu.make_async_remote_copy(
            src_ref=theirs.at[i], dst_ref=mbuf.at[i], send_sem=msend_sem.at[i], recv_sem=mrecv_sem.at[i],
            device_id=(partner, my), device_id_type=MESH)
        copy.start()
        crossing[i] = copy

    def finish(i):
        if i in HALVED:
            crossing[i].wait_recv()
            mine[i] += mbuf[i].astype(jnp.float32)
        else:
            mine[i] = add_up(i)

    for kind, *where in ORDER:
        {"launch": launch, "weights": weights, "multiply": multiply, "combine": combine, "cross": cross, "finish": finish}[kind](*where)

    want = jnp.full((TILE, TILE), (lv[my] ^ cj[me]) * 8, jnp.int32)
    for v in range(ntiles):
        found = jnp.zeros((TILE, TILE), jnp.float32)
        for i in range(min(v + 1, SLOTS)):
            found = jnp.where(want == codes[v] - i, mine[i], found)
        out[:, v * TILE:(v + 1) * TILE] = found.astype(out.dtype)

    for i in range(SLOTS):
        sent = pk.at[i, pl.ds(0, n_tile - 2 if i in HALVED else n_tile - 1)]
        pltpu.make_async_copy(sent, sent, send_sem.at[i]).wait()
        if i not in TWO_STEP:
            sent = part[i].at[pl.ds(0, n_red - 1)]
            pltpu.make_async_copy(sent, sent, ysend_sem.at[i, 0]).wait()
    for copy in list(hops.values()) + list(crossing.values()):
        copy.wait_send()


def local(n_tile, n_red, amplitudes, intermediate, contract_irrep, column_irrep, virtual_irrep):
    n_k, n_j, rows, width = amplitudes.shape
    dims = (4, 8, 2)
    bf = jnp.bfloat16
    smem = pl.BlockSpec(memory_space=pltpu.SMEM)
    hbm = pl.BlockSpec(memory_space=pl.ANY)
    cols = [2 * TILE if i in HALVED else TILE for i in range(SLOTS)]
    blocks = [pltpu.VMEM((n_red, TILE, c), bf) for c in cols]
    out = pl.pallas_call(
        functools.partial(kernel, dims, n_tile, n_red),
        out_shape=jax.ShapeDtypeStruct((TILE, width), bf),
        in_specs=[smem, smem, smem, hbm, hbm],
        out_specs=pl.BlockSpec(memory_space=pltpu.VMEM),
        scratch_shapes=[
            pltpu.VMEM((n_k, n_j, rows, width), bf),
            pltpu.VMEM((width, n_k, width), bf),
            pltpu.VMEM((n_k, width, width), bf),
            pltpu.VMEM((8, width), jnp.int32),
            pltpu.VMEM((SLOTS, n_j, n_k, rows, TILE), bf),
            [pltpu.VMEM((n_k, width, c), bf) for c in cols],
            blocks,
            blocks,
            pltpu.VMEM((SLOTS, TILE, TILE), jnp.float32),
            pltpu.VMEM((SLOTS, TILE, TILE), bf),
            pltpu.VMEM((SLOTS, TILE, TILE), bf),
            blocks,
            pltpu.SemaphoreType.DMA,
            pltpu.SemaphoreType.DMA,
            pltpu.SemaphoreType.DMA((SLOTS,)),
            pltpu.SemaphoreType.DMA((SLOTS,)),
            pltpu.SemaphoreType.DMA((SLOTS, 2)),
            pltpu.SemaphoreType.DMA((SLOTS, n_red)),
            pltpu.SemaphoreType.DMA((SLOTS, n_red)),
            pltpu.SemaphoreType.DMA((SLOTS,)),
            pltpu.SemaphoreType.DMA((SLOTS,)),
        ],
        compiler_params=pltpu.CompilerParams(
            collective_id=0, has_side_effects=True, vmem_limit_bytes=59 * 2**20
        ),
        cost_estimate=pl.CostEstimate(flops=2 * width**2 * n_k * SLOTS * TILE, bytes_accessed=9 * 2**20,
                                      transcendentals=0),
    )(contract_irrep, column_irrep, virtual_irrep, amplitudes, intermediate)
    return out[:, None, :]


def solution(mesh):
    in_specs = (P("red", None, "tile", None), P(None, "red", None), P("red"), P(), P())
    out_specs = P("red", "tile", None)
    body = functools.partial(local, mesh.shape["tile"], mesh.shape["red"])
    return jax.shard_map(body, mesh=mesh, in_specs=in_specs, out_specs=out_specs, check_vma=False)
```

```python
import functools

import jax
import jax.numpy as jnp
from jax import lax
from jax.experimental import pallas as pl
from jax.experimental.pallas import tpu as pltpu
from jax.sharding import PartitionSpec as P

TILE = 128
SLOTS = 4
HALVED = (0, 1, 2)
TWO_STEP = (0, 1, 2, 3)
ORDER = (
    ("launch", 0), ("launch", 1), ("launch", 2), ("launch", 3), ("weights",),
    ("multiply", 0), ("combine", 0), ("multiply", 1), ("combine", 1), ("cross", 0),
    ("multiply", 2), ("combine", 2), ("cross", 1), ("multiply", 3), ("cross", 2),
    ("combine", 3), ("finish", 0), ("finish", 1), ("finish", 2), ("finish", 3),
)
MESH = pl.DeviceIdType.MESH


def wrap(value, size):
    return jnp.where(value >= size, value - size, value)


def tile_codes(lv, ntiles):
    codes = []
    for v in range(ntiles):
        code = lv[v] * 8
        for u in range(v):
            code = code + (lv[u] == lv[v]).astype(jnp.int32)
        codes.append(code)
    return codes


def kernel(dims, n_tile, n_red, ck, cj, lv, t_hbm, w_hbm, out, tv, wraw, wv, lanes, pk, recv, part, ybuf, mine, theirs, mbuf, sums,
           t_sem, w_sem, send_sem, recv_sem, own_sem, ysend_sem, yrecv_sem, msend_sem, mrecv_sem):
    xs, zs, cs = dims
    me, my = lax.axis_index("tile"), lax.axis_index("red")
    n_k, n_j, rows, width = tv.shape
    ntiles = width // TILE
    half = zs // 2
    core, z, x = me % cs, (me // cs) % zs, me // (cs * zs)
    partner = (x * zs + wrap(z + half, zs)) * cs + core

    steps = [(dcore, dz) for dz in (1, zs - 1, half, 2, zs - 2, 0, 3, zs - 3) for dcore in range(cs)]
    places, homes = [], []
    for dcore, dz in steps:
        j_core, j_z = wrap(core + dcore, cs), wrap(z + dz, zs)
        behind = wrap(zs - dz + 2 - j_core, zs)
        across = jnp.where(behind >= half, 1, 0)
        places.append(j_z * cs + j_core)
        homes.append((wrap(j_z + half * across, zs) * cs + j_core, across))

    planes = [wrap(x + dx, xs) * zs * cs for dx in range(xs)]

    def each_peer(visit, skip):
        for q in range(len(steps)):
            for dx in range(xs):
                if dx or steps[q] not in skip:
                    visit(planes[dx], q)

    t_copy = pltpu.make_async_copy(t_hbm, tv, t_sem)
    t_copy.start()
    w_copy = pltpu.make_async_copy(w_hbm, wraw, w_sem)
    w_copy.start()

    barrier = pltpu.get_barrier_semaphore()

    def greet(base, q):
        pl.semaphore_signal(barrier, inc=1, device_id=(base + places[q], my), device_id_type=MESH)

    each_peer(greet, [(0, 0)])
    for d in (1, 2, n_red - 2, n_red - 1):
        pl.semaphore_signal(barrier, inc=1, device_id=(me, wrap(my + d, n_red)), device_id_type=MESH)

    def clear(n, carry):
        for far in range(half):
            first = (n * zs + wrap(z + wrap(half - 2 + core + far, zs), zs)) * cs * rows
            where = pl.ds(pl.multiple_of(first, cs * rows), cs * rows)
            for i in HALVED:
                for k in range(n_k):
                    recv[i][k, where, :] = jnp.zeros((cs * rows, 2 * TILE), recv[i].dtype)
        return carry

    lax.fori_loop(0, xs, clear, 0)

    codes = tile_codes(lv, ntiles)
    own_label = lv[me * rows // TILE]
    for c in range(ntiles):
        lanes[:, c * TILE:(c + 1) * TILE] = jnp.full((8, TILE), lv[c], jnp.int32)
    t_copy.wait()

    def pack(j, carry):
        for k in range(n_k):
            key = jnp.full((rows, TILE), (ck[k] ^ cj[j] ^ own_label) * 8, jnp.int32)
            tiles = [tv[k, j, :, v * TILE:(v + 1) * TILE].astype(jnp.float32) for v in range(ntiles)]
            for i in range(SLOTS):
                found = tiles[i]
                for v in range(i + 1, ntiles):
                    found = jnp.where(key == codes[v] - i, tiles[v], found)
                pk[i, j, k] = found.astype(pk.dtype)
        return carry

    lax.fori_loop(0, n_j, pack, 0)
    pl.semaphore_wait(barrier, n_tile - 1 + 4)

    own_rows = pl.ds(pl.multiple_of(me * rows, rows), rows)
    own = {}

    def send(i, base, q):
        place, (home, across) = places[q], homes[q]
        if i in HALVED:
            to = base + home
            columns = pl.ds(pl.multiple_of(across * TILE, TILE), TILE)
        else:
            to = base + place
            columns = pl.ds(0, TILE)
        pltpu.make_async_remote_copy(
            src_ref=pk.at[i, base + place],
            dst_ref=recv[i].at[:, own_rows, columns],
            send_sem=send_sem.at[i],
            recv_sem=recv_sem.at[i],
            device_id=(to, my),
            device_id_type=MESH,
        ).start()

    def launch(i):
        copies = [pltpu.make_async_copy(pk.at[i, me], recv[i].at[:, own_rows, pl.ds(0, TILE)], own_sem.at[i, 0])]
        if i in HALVED:
            each_peer(functools.partial(send, i), [(0, 0), (0, half)])
            copies.append(pltpu.make_async_copy(
                pk.at[i, partner], recv[i].at[:, own_rows, pl.ds(TILE, TILE)], own_sem.at[i, 1]))
        else:
            each_peer(functools.partial(send, i), [(0, 0)])
        for copy in copies:
            copy.start()
        own[i] = copies

    def weights():
        w_copy.wait()
        row = lax.broadcasted_iota(jnp.int32, (TILE, n_k * TILE), 0)
        col = lax.broadcasted_iota(jnp.int32, (TILE, n_k * TILE), 1)
        picks = [jnp.where(col == n_k * row + k, 1.0, 0.0).astype(wv.dtype) for k in range(n_k)]

        def arrange(a, carry):
            a_rows = pl.ds(pl.multiple_of(a * TILE, TILE), TILE)
            pairs = wraw[a_rows].reshape(n_k * TILE, width)
            for k in range(n_k):
                plane = jnp.dot(picks[k], pairs, preferred_element_type=jnp.float32)
                keep = jnp.broadcast_to(lanes[0:1, :], plane.shape) == jnp.full(plane.shape, lv[a] ^ ck[k], jnp.int32)
                wv[k, a_rows, :] = jnp.where(keep, plane, 0.0).astype(wv.dtype)
            return carry

        lax.fori_loop(0, ntiles, arrange, 0)

    def along(offset):
        offset = offset % n_red
        return wrap(my + jnp.where(core == 1, n_red - offset, offset), n_red)

    first_step = ((0, -3, -1), (1, 4, 2), (2, 3, 1), (3, -1, -1), (4, 1, 1))

    def hop(i, slot, block, offset):
        return pltpu.make_async_remote_copy(
            src_ref=block,
            dst_ref=ybuf[i].at[slot],
            send_sem=ysend_sem.at[i, slot],
            recv_sem=yrecv_sem.at[i, slot],
            device_id=(me, along(offset)),
            device_id_type=MESH,
        )

    hops = {}
    first_pair = wrap(my // 2 + n_red // 4, n_red // 2)

    def multiply(i):
        for copy in own[i]:
            copy.wait()
        n_got = n_tile - 2 if i in HALVED else n_tile - 1
        others = recv[i].at[:, pl.ds(0, n_got * rows), pl.ds(0, TILE)]
        pltpu.make_async_copy(others, others, recv_sem.at[i]).wait()

        def block(n, carry):
            pair = wrap(first_pair + n, n_red // 2)
            a_rows = pl.ds(pl.multiple_of(pair * 2 * TILE, 2 * TILE), 2 * TILE)
            acc = jnp.dot(wv[0, a_rows, :], recv[i][0], preferred_element_type=jnp.float32)
            for k in range(1, n_k):
                acc += jnp.dot(wv[k, a_rows, :], recv[i][k], preferred_element_type=jnp.float32)
            for h in range(2):
                to = pair * 2 + h
                part[i][to] = acc[h * TILE:(h + 1) * TILE].astype(part[i].dtype)

                if i not in TWO_STEP:
                    @pl.when(to != my)
                    def _():
                        pltpu.make_async_remote_copy(
                            src_ref=part[i].at[to],
                            dst_ref=ybuf[i].at[my],
                            send_sem=ysend_sem.at[i, 0],
                            recv_sem=yrecv_sem.at[i, 0],
                            device_id=(me, to),
                            device_id_type=MESH,
                        ).start()
            return carry

        lax.fori_loop(0, n_red // 2, block, 0)
        if i in TWO_STEP:
            for slot, to, by in first_step:
                hops[i, slot] = hop(i, slot, part[i].at[along(to)], by)
                hops[i, slot].start()

    def combine(i):
        for slot, to, parts in ((5, -2, (0,)), (6, 2, (1, 2))):
            total = part[i][along(to)].astype(jnp.float32)
            for p in parts:
                hops[i, p].wait_recv()
                total += ybuf[i][p].astype(jnp.float32)
            sums[i][slot] = total.astype(sums[i].dtype)
            hops[i, slot] = hop(i, slot, sums[i].at[slot], to)
            hops[i, slot].start()

    def add_up(i):
        total = part[i][my].astype(jnp.float32)
        if i in TWO_STEP:
            for slot in (3, 4, 5, 6):
                hops[i, slot].wait_recv()
                total += ybuf[i][slot].astype(jnp.float32)
        else:
            others = ybuf[i].at[pl.ds(0, n_red - 1)]
            pltpu.make_async_copy(others, others, yrecv_sem.at[i, 0]).wait()
            for d in range(1, n_red):
                total += ybuf[i][wrap(my + d, n_red)].astype(jnp.float32)
        return total

    crossing = {}

    def cross(i):
        total = add_up(i)
        mine[i] = total[:, :TILE]
        theirs[i] = total[:, TILE:].astype(theirs.dtype)
        copy = pltpu.make_async_remote_copy(
            src_ref=theirs.at[i], dst_ref=mbuf.at[i], send_sem=msend_sem.at[i], recv_sem=mrecv_sem.at[i],
            device_id=(partner, my), device_id_type=MESH)
        copy.start()
        crossing[i] = copy

    def finish(i):
        if i in HALVED:
            crossing[i].wait_recv()
            mine[i] += mbuf[i].astype(jnp.float32)
        else:
            mine[i] = add_up(i)

    for kind, *where in ORDER:
        {"launch": launch, "weights": weights, "multiply": multiply, "combine": combine, "cross": cross, "finish": finish}[kind](*where)

    want = jnp.full((TILE, TILE), (lv[my] ^ cj[me]) * 8, jnp.int32)
    for v in range(ntiles):
        found = jnp.zeros((TILE, TILE), jnp.float32)
        for i in range(min(v + 1, SLOTS)):
            found = jnp.where(want == codes[v] - i, mine[i], found)
        out[:, v * TILE:(v + 1) * TILE] = found.astype(out.dtype)

    for i in range(SLOTS):
        sent = pk.at[i, pl.ds(0, n_tile - 2 if i in HALVED else n_tile - 1)]
        pltpu.make_async_copy(sent, sent, send_sem.at[i]).wait()
        if i not in TWO_STEP:
            sent = part[i].at[pl.ds(0, n_red - 1)]
            pltpu.make_async_copy(sent, sent, ysend_sem.at[i, 0]).wait()
    for copy in list(hops.values()) + list(crossing.values()):
        copy.wait_send()


def local(n_tile, n_red, amplitudes, intermediate, contract_irrep, column_irrep, virtual_irrep):
    n_k, n_j, rows, width = amplitudes.shape
    dims = (4, 8, 2)
    bf = jnp.bfloat16
    smem = pl.BlockSpec(memory_space=pltpu.SMEM)
    hbm = pl.BlockSpec(memory_space=pl.ANY)
    cols = [2 * TILE if i in HALVED else TILE for i in range(SLOTS)]
    blocks = [pltpu.VMEM((n_red, TILE, c), bf) for c in cols]
    out = pl.pallas_call(
        functools.partial(kernel, dims, n_tile, n_red),
        out_shape=jax.ShapeDtypeStruct((TILE, width), bf),
        in_specs=[smem, smem, smem, hbm, hbm],
        out_specs=pl.BlockSpec(memory_space=pltpu.VMEM),
        scratch_shapes=[
            pltpu.VMEM((n_k, n_j, rows, width), bf),
            pltpu.VMEM((width, n_k, width), bf),
            pltpu.VMEM((n_k, width, width), bf),
            pltpu.VMEM((8, width), jnp.int32),
            pltpu.VMEM((SLOTS, n_j, n_k, rows, TILE), bf),
            [pltpu.VMEM((n_k, width, c), bf) for c in cols],
            blocks,
            blocks,
            pltpu.VMEM((SLOTS, TILE, TILE), jnp.float32),
            pltpu.VMEM((SLOTS, TILE, TILE), bf),
            pltpu.VMEM((SLOTS, TILE, TILE), bf),
            blocks,
            pltpu.SemaphoreType.DMA,
            pltpu.SemaphoreType.DMA,
            pltpu.SemaphoreType.DMA((SLOTS,)),
            pltpu.SemaphoreType.DMA((SLOTS,)),
            pltpu.SemaphoreType.DMA((SLOTS, 2)),
            pltpu.SemaphoreType.DMA((SLOTS, n_red)),
            pltpu.SemaphoreType.DMA((SLOTS, n_red)),
            pltpu.SemaphoreType.DMA((SLOTS,)),
            pltpu.SemaphoreType.DMA((SLOTS,)),
        ],
        compiler_params=pltpu.CompilerParams(
            collective_id=0, has_side_effects=True, vmem_limit_bytes=59 * 2**20
        ),
        cost_estimate=pl.CostEstimate(flops=2 * width**2 * n_k * SLOTS * TILE, bytes_accessed=9 * 2**20,
                                      transcendentals=0),
    )(contract_irrep, column_irrep, virtual_irrep, amplitudes, intermediate)
    return out[:, None, :]


def solution(mesh):
    in_specs = (P("red", None, "tile", None), P(None, "red", None), P("red"), P(), P())
    out_specs = P("red", "tile", None)
    body = functools.partial(local, mesh.shape["tile"], mesh.shape["red"])
    return jax.shard_map(body, mesh=mesh, in_specs=in_specs, out_specs=out_specs, check_vma=False)
```

```python
import functools

import jax
import jax.numpy as jnp
from jax import lax
from jax.experimental import pallas as pl
from jax.experimental.pallas import tpu as pltpu
from jax.sharding import PartitionSpec as P

TILE = 128
SLOTS = 4
HALVED = (0, 1, 2)
TWO_STEP = (0, 1, 2, 3)
ORDER = (
    ("launch", 0), ("launch", 1), ("launch", 2), ("launch", 3), ("weights",),
    ("multiply", 0), ("combine", 0), ("multiply", 1), ("combine", 1), ("cross", 0),
    ("multiply", 2), ("combine", 2), ("cross", 1), ("multiply", 3), ("cross", 2),
    ("combine", 3), ("finish", 0), ("finish", 1), ("finish", 2), ("finish", 3),
)
MESH = pl.DeviceIdType.MESH


def wrap(value, size):
    return jnp.where(value >= size, value - size, value)


def tile_codes(lv, ntiles):
    codes = []
    for v in range(ntiles):
        code = lv[v] * 8
        for u in range(v):
            code = code + (lv[u] == lv[v]).astype(jnp.int32)
        codes.append(code)
    return codes


def kernel(dims, n_tile, n_red, ck, cj, lv, t_hbm, w_hbm, out, tv, wraw, wv, lanes, pk, recv, part, ybuf, mine, theirs, mbuf, sums,
           t_sem, w_sem, send_sem, recv_sem, own_sem, ysend_sem, yrecv_sem, msend_sem, mrecv_sem):
    xs, zs, cs = dims
    me, my = lax.axis_index("tile"), lax.axis_index("red")
    n_k, n_j, rows, width = tv.shape
    ntiles = width // TILE
    half = zs // 2
    core, z, x = me % cs, (me // cs) % zs, me // (cs * zs)
    partner = (x * zs + wrap(z + half, zs)) * cs + core

    steps = [(dcore, dz) for dz in (1, zs - 1, half, 2, zs - 2, 0, 3, zs - 3) for dcore in range(cs)]
    places, homes = [], []
    for dcore, dz in steps:
        j_core, j_z = wrap(core + dcore, cs), wrap(z + dz, zs)
        behind = wrap(zs - dz + 2 - j_core, zs)
        across = jnp.where(behind >= half, 1, 0)
        places.append(j_z * cs + j_core)
        homes.append((wrap(j_z + half * across, zs) * cs + j_core, across))

    planes = [wrap(x + dx, xs) * zs * cs for dx in range(xs)]

    def each_peer(visit, skip):
        for q in range(len(steps)):
            for dx in range(xs):
                if dx or steps[q] not in skip:
                    visit(planes[dx], q)

    t_copy = pltpu.make_async_copy(t_hbm, tv, t_sem)
    t_copy.start()
    w_copy = pltpu.make_async_copy(w_hbm, wraw, w_sem)
    w_copy.start()

    barrier = pltpu.get_barrier_semaphore()

    def greet(base, q):
        pl.semaphore_signal(barrier, inc=1, device_id=(base + places[q], my), device_id_type=MESH)

    each_peer(greet, [(0, 0)])
    for d in (1, 2, n_red - 2, n_red - 1):
        pl.semaphore_signal(barrier, inc=1, device_id=(me, wrap(my + d, n_red)), device_id_type=MESH)

    def clear(n, carry):
        for far in range(half):
            first = (n * zs + wrap(z + wrap(half - 2 + core + far, zs), zs)) * cs * rows
            where = pl.ds(pl.multiple_of(first, cs * rows), cs * rows)
            for i in HALVED:
                for k in range(n_k):
                    recv[i][k, where, :] = jnp.zeros((cs * rows, 2 * TILE), recv[i].dtype)
        return carry

    lax.fori_loop(0, xs, clear, 0)

    codes = tile_codes(lv, ntiles)
    own_label = lv[me * rows // TILE]
    for c in range(ntiles):
        lanes[:, c * TILE:(c + 1) * TILE] = jnp.full((8, TILE), lv[c], jnp.int32)
    t_copy.wait()

    def pack(j, carry):
        for k in range(n_k):
            key = jnp.full((rows, TILE), (ck[k] ^ cj[j] ^ own_label) * 8, jnp.int32)
            tiles = [tv[k, j, :, v * TILE:(v + 1) * TILE].astype(jnp.float32) for v in range(ntiles)]
            for i in range(SLOTS):
                found = tiles[i]
                for v in range(i + 1, ntiles):
                    found = jnp.where(key == codes[v] - i, tiles[v], found)
                pk[i, j, k] = found.astype(pk.dtype)
        return carry

    lax.fori_loop(0, n_j, pack, 0)
    pl.semaphore_wait(barrier, n_tile - 1 + 4)

    own_rows = pl.ds(pl.multiple_of(me * rows, rows), rows)
    own = {}

    def send(i, base, q):
        place, (home, across) = places[q], homes[q]
        if i in HALVED:
            to = base + home
            columns = pl.ds(pl.multiple_of(across * TILE, TILE), TILE)
        else:
            to = base + place
            columns = pl.ds(0, TILE)
        pltpu.make_async_remote_copy(
            src_ref=pk.at[i, base + place],
            dst_ref=recv[i].at[:, own_rows, columns],
            send_sem=send_sem.at[i],
            recv_sem=recv_sem.at[i],
            device_id=(to, my),
            device_id_type=MESH,
        ).start()

    def launch(i):
        copies = [pltpu.make_async_copy(pk.at[i, me], recv[i].at[:, own_rows, pl.ds(0, TILE)], own_sem.at[i, 0])]
        if i in HALVED:
            each_peer(functools.partial(send, i), [(0, 0), (0, half)])
            copies.append(pltpu.make_async_copy(
                pk.at[i, partner], recv[i].at[:, own_rows, pl.ds(TILE, TILE)], own_sem.at[i, 1]))
        else:
            each_peer(functools.partial(send, i), [(0, 0)])
        for copy in copies:
            copy.start()
        own[i] = copies

    def weights():
        w_copy.wait()
        row = lax.broadcasted_iota(jnp.int32, (TILE, n_k * TILE), 0)
        col = lax.broadcasted_iota(jnp.int32, (TILE, n_k * TILE), 1)
        picks = [jnp.where(col == n_k * row + k, 1.0, 0.0).astype(wv.dtype) for k in range(n_k)]

        def arrange(a, carry):
            a_rows = pl.ds(pl.multiple_of(a * TILE, TILE), TILE)
            pairs = wraw[a_rows].reshape(n_k * TILE, width)
            for k in range(n_k):
                plane = jnp.dot(picks[k], pairs, preferred_element_type=jnp.float32)
                keep = jnp.broadcast_to(lanes[0:1, :], plane.shape) == jnp.full(plane.shape, lv[a] ^ ck[k], jnp.int32)
                wv[k, a_rows, :] = jnp.where(keep, plane, 0.0).astype(wv.dtype)
            return carry

        lax.fori_loop(0, ntiles, arrange, 0)

    def along(offset):
        offset = offset % n_red
        return wrap(my + jnp.where(core == 1, n_red - offset, offset), n_red)

    first_step = ((0, -3, -1), (1, 4, 2), (2, 3, 1), (3, -1, -1), (4, 1, 1))

    def hop(i, slot, block, offset):
        return pltpu.make_async_remote_copy(
            src_ref=block,
            dst_ref=ybuf[i].at[slot],
            send_sem=ysend_sem.at[i, slot],
            recv_sem=yrecv_sem.at[i, slot],
            device_id=(me, along(offset)),
            device_id_type=MESH,
        )

    hops = {}
    first_pair = wrap(my // 2 + n_red // 4, n_red // 2)
    beside = jnp.where(my - my // 2 * 2 == 1, 1, n_red // 2 - 1)

    def multiply(i):
        for copy in own[i]:
            copy.wait()
        n_got = n_tile - 2 if i in HALVED else n_tile - 1
        others = recv[i].at[:, pl.ds(0, n_got * rows), pl.ds(0, TILE)]
        pltpu.make_async_copy(others, others, recv_sem.at[i]).wait()

        def block(n):
            pair = wrap(first_pair + n, n_red // 2)
            a_rows = pl.ds(pl.multiple_of(pair * 2 * TILE, 2 * TILE), 2 * TILE)
            acc = jnp.dot(wv[0, a_rows, :], recv[i][0], preferred_element_type=jnp.float32)
            for k in range(1, n_k):
                acc += jnp.dot(wv[k, a_rows, :], recv[i][k], preferred_element_type=jnp.float32)
            for h in range(2):
                to = pair * 2 + h
                part[i][to] = acc[h * TILE:(h + 1) * TILE].astype(part[i].dtype)

                if i not in TWO_STEP:
                    @pl.when(to != my)
                    def _():
                        pltpu.make_async_remote_copy(
                            src_ref=part[i].at[to],
                            dst_ref=ybuf[i].at[my],
                            send_sem=ysend_sem.at[i, 0],
                            recv_sem=yrecv_sem.at[i, 0],
                            device_id=(me, to),
                            device_id_type=MESH,
                        ).start()

        def near(n, carry):
            block(n * beside)
            return carry

        def rest(n, carry):
            other = n_red // 2 - beside
            block(other + n * (2 - other))
            return carry

        lax.fori_loop(0, 2, near, 0)
        if i in TWO_STEP:
            depart(i, first_step[:3])
        lax.fori_loop(0, 2, rest, 0)
        if i in TWO_STEP:
            depart(i, first_step[3:])

    def depart(i, which):
        for slot, to, by in which:
            hops[i, slot] = hop(i, slot, part[i].at[along(to)], by)
            hops[i, slot].start()

    def combine(i):
        for slot, to, parts in ((5, -2, (0,)), (6, 2, (1, 2))):
            total = part[i][along(to)].astype(jnp.float32)
            for p in parts:
                hops[i, p].wait_recv()
                total += ybuf[i][p].astype(jnp.float32)
            sums[i][slot] = total.astype(sums[i].dtype)
            hops[i, slot] = hop(i, slot, sums[i].at[slot], to)
            hops[i, slot].start()

    def add_up(i):
        total = part[i][my].astype(jnp.float32)
        if i in TWO_STEP:
            for slot in (3, 4, 5, 6):
                hops[i, slot].wait_recv()
                total += ybuf[i][slot].astype(jnp.float32)
        else:
            others = ybuf[i].at[pl.ds(0, n_red - 1)]
            pltpu.make_async_copy(others, others, yrecv_sem.at[i, 0]).wait()
            for d in range(1, n_red):
                total += ybuf[i][wrap(my + d, n_red)].astype(jnp.float32)
        return total

    crossing = {}

    def cross(i):
        total = add_up(i)
        mine[i] = total[:, :TILE]
        theirs[i] = total[:, TILE:].astype(theirs.dtype)
        copy = pltpu.make_async_remote_copy(
            src_ref=theirs.at[i], dst_ref=mbuf.at[i], send_sem=msend_sem.at[i], recv_sem=mrecv_sem.at[i],
            device_id=(partner, my), device_id_type=MESH)
        copy.start()
        crossing[i] = copy

    def finish(i):
        if i in HALVED:
            crossing[i].wait_recv()
            mine[i] += mbuf[i].astype(jnp.float32)
        else:
            mine[i] = add_up(i)

    for kind, *where in ORDER:
        {"launch": launch, "weights": weights, "multiply": multiply, "combine": combine, "cross": cross, "finish": finish}[kind](*where)

    want = jnp.full((TILE, TILE), (lv[my] ^ cj[me]) * 8, jnp.int32)
    for v in range(ntiles):
        found = jnp.zeros((TILE, TILE), jnp.float32)
        for i in range(min(v + 1, SLOTS)):
            found = jnp.where(want == codes[v] - i, mine[i], found)
        out[:, v * TILE:(v + 1) * TILE] = found.astype(out.dtype)

    for i in range(SLOTS):
        sent = pk.at[i, pl.ds(0, n_tile - 2 if i in HALVED else n_tile - 1)]
        pltpu.make_async_copy(sent, sent, send_sem.at[i]).wait()
        if i not in TWO_STEP:
            sent = part[i].at[pl.ds(0, n_red - 1)]
            pltpu.make_async_copy(sent, sent, ysend_sem.at[i, 0]).wait()
    for copy in list(hops.values()) + list(crossing.values()):
        copy.wait_send()


def local(n_tile, n_red, amplitudes, intermediate, contract_irrep, column_irrep, virtual_irrep):
    n_k, n_j, rows, width = amplitudes.shape
    dims = (4, 8, 2)
    bf = jnp.bfloat16
    smem = pl.BlockSpec(memory_space=pltpu.SMEM)
    hbm = pl.BlockSpec(memory_space=pl.ANY)
    cols = [2 * TILE if i in HALVED else TILE for i in range(SLOTS)]
    blocks = [pltpu.VMEM((n_red, TILE, c), bf) for c in cols]
    out = pl.pallas_call(
        functools.partial(kernel, dims, n_tile, n_red),
        out_shape=jax.ShapeDtypeStruct((TILE, width), bf),
        in_specs=[smem, smem, smem, hbm, hbm],
        out_specs=pl.BlockSpec(memory_space=pltpu.VMEM),
        scratch_shapes=[
            pltpu.VMEM((n_k, n_j, rows, width), bf),
            pltpu.VMEM((width, n_k, width), bf),
            pltpu.VMEM((n_k, width, width), bf),
            pltpu.VMEM((8, width), jnp.int32),
            pltpu.VMEM((SLOTS, n_j, n_k, rows, TILE), bf),
            [pltpu.VMEM((n_k, width, c), bf) for c in cols],
            blocks,
            blocks,
            pltpu.VMEM((SLOTS, TILE, TILE), jnp.float32),
            pltpu.VMEM((SLOTS, TILE, TILE), bf),
            pltpu.VMEM((SLOTS, TILE, TILE), bf),
            blocks,
            pltpu.SemaphoreType.DMA,
            pltpu.SemaphoreType.DMA,
            pltpu.SemaphoreType.DMA((SLOTS,)),
            pltpu.SemaphoreType.DMA((SLOTS,)),
            pltpu.SemaphoreType.DMA((SLOTS, 2)),
            pltpu.SemaphoreType.DMA((SLOTS, n_red)),
            pltpu.SemaphoreType.DMA((SLOTS, n_red)),
            pltpu.SemaphoreType.DMA((SLOTS,)),
            pltpu.SemaphoreType.DMA((SLOTS,)),
        ],
        compiler_params=pltpu.CompilerParams(
            collective_id=0, has_side_effects=True, vmem_limit_bytes=59 * 2**20
        ),
        cost_estimate=pl.CostEstimate(flops=2 * width**2 * n_k * SLOTS * TILE, bytes_accessed=9 * 2**20,
                                      transcendentals=0),
    )(contract_irrep, column_irrep, virtual_irrep, amplitudes, intermediate)
    return out[:, None, :]


def solution(mesh):
    in_specs = (P("red", None, "tile", None), P(None, "red", None), P("red"), P(), P())
    out_specs = P("red", "tile", None)
    body = functools.partial(local, mesh.shape["tile"], mesh.shape["red"])
    return jax.shard_map(body, mesh=mesh, in_specs=in_specs, out_specs=out_specs, check_vma=False)
```
